32 devices in a mesh: row: 8 (over y, x, core), col: 4 (over z).
Axes of the slice: x: 2, y: 2, z: 4, core: 2. Of those that a mesh axis runs over, the one named last changes fastest.
Arguments:
- field_in: bfloat16 [256, 256, 256], P('row', 'col'), may hold values from -40 to 40
- cotangent: bfloat16 [256, 256, 256], P('row', 'col'), may hold values from -6 to 6
- gain_conv: float32 [256], replicated, may hold values from 0.1 to 1.9
- w_expand: bfloat16 [256, 1024], replicated, may hold values from -0.375 to 0.375
- w_depth: float32 [3, 3, 1024], replicated, may hold values from -4 to 4
- w_project: bfloat16 [1024, 256], replicated, may hold values from -0.1875 to 0.1875
- gain_attn: float32 [256], replicated, may hold values from 0.1 to 1.9
- w_qkv: bfloat16 [256, 768], replicated, may hold values from -1.25 to 1.25
- w_out: bfloat16 [256, 256], replicated, may hold values from -0.375 to 0.375
Outputs:
- grad_field: bfloat16 [256, 256, 256], P('row', 'col')
- grad_gain_conv: float32 [256], replicated
- grad_expand: float32 [256, 1024], replicated
- grad_depth: float32 [3, 3, 1024], replicated
- grad_project: float32 [1024, 256], replicated
- grad_gain_attn: float32 [256], replicated
- grad_qkv: float32 [256, 768], replicated
- grad_out: float32 [256, 256], replicated
The draws below stay inside these ranges and needn't reach their ends.
All inputs are finite; a program needn't handle non-finite values.
Results may differ from the reference program's by a relative error of at most 0.025.
The reference program's roundings to bfloat16 on the way count: a program that leaves them out, or rounds other values in their place, can miss the bound.
Values may be sent and summed in bfloat16 or wider, within the bound.
A program may use at most 192 MiB of HBM per device.

```python
import math
import jax
import jax.numpy as jnp
from jax import lax

WIDTH = 256
HEADS = 8
EXPANDED = 1024
GRID = 16
FIELD_ROWS = 256
FIELD_COLS = 256
TOKENS = 65536


def draw_field_in(key, part):
    streams = jax.random.split(jax.random.fold_in(key, 11), 3)
    noise = jnp.clip(jax.random.normal(streams[0], (FIELD_ROWS, FIELD_COLS, WIDTH), jnp.float32), -4.0, 4.0)
    token_scale = jnp.exp(jax.random.uniform(streams[1], (FIELD_ROWS, FIELD_COLS, 1), jnp.float32) * math.log(10.0))
    chan_scale = jnp.exp(jax.random.uniform(streams[2], (WIDTH,), jnp.float32) * math.log(10.0))
    return (noise * token_scale * chan_scale * 0.1).astype(jnp.bfloat16)


def draw_w_qkv(key, part):
    streams = jax.random.split(jax.random.fold_in(key, 23), 1)
    weights = jnp.clip(jax.random.normal(streams[0], (WIDTH, 3 * WIDTH), jnp.float32), -4.0, 4.0) * WIDTH ** (-0.5)
    return weights.astype(jnp.bfloat16)


def steps_of(own_key, shape, cuts, smallest, top_value):
    def one(position, blocks):
        heights = jax.random.uniform(jax.random.fold_in(jax.random.fold_in(own_key, 6), position), (blocks,), jnp.float32, smallest / len(cuts), top_value / len(cuts))
        return jnp.repeat(jnp.exp(heights), shape[position] // blocks).reshape((-1,) + (1,) * (len(shape) - position - 1))

    level = one(*cuts[0])
    for cut in cuts[1:]:
        level = level * one(*cut)
    return level


def normal_values(key, shape, scale, limit, shards=(), kind=jnp.bfloat16):
    gain = steps_of(key, shape, shards, -0.22, 0.18) if shards else 1.0
    result = jax.random.normal(key, shape, jnp.float32) * scale * gain
    return jnp.minimum(jnp.maximum(result, -limit), limit).astype(kind)


def setup_inputs(seed: int = 0) -> dict:
    splits = jax.random.split(jax.random.key(seed), 10)
    return {
        "field_in": draw_field_in(jax.random.fold_in(splits[9], 71), 0),
        "cotangent": normal_values(splits[1], (FIELD_ROWS, FIELD_COLS, WIDTH), 1.0, 6.0, ((0, 8), (1, 4))),
        "gain_conv": jnp.clip(1.0 + 0.18 * jax.random.normal(splits[2], (WIDTH,), jnp.float32), 0.1, 1.9),
        "w_expand": normal_values(splits[3], (WIDTH, EXPANDED), WIDTH ** -0.5, 0.375),
        "w_depth": normal_values(splits[4], (3, 3, EXPANDED), 1.0, 4.0, (), jnp.float32),
        "w_project": normal_values(splits[5], (EXPANDED, WIDTH), EXPANDED ** -0.5, 0.1875),
        "gain_attn": jnp.clip(1.0 + 0.18 * jax.random.normal(splits[6], (WIDTH,), jnp.float32), 0.1, 1.9),
        "w_qkv": draw_w_qkv(jax.random.fold_in(splits[9], 71), 0),
        "w_out": normal_values(splits[8], (WIDTH, WIDTH), WIDTH ** -0.5, 0.375),
    }


norm_eps = 1e-05
root_half = 0.7071067811865476
inv_root_two_pi = 0.3989422804014327

def gelu_value(values):
    return 0.5 * values * (1.0 + lax.erf(values * root_half))

def gelu_slope(values):
    return 0.5 * (1.0 + lax.erf(values * root_half)) + values * jnp.exp(-0.5 * values * values) * inv_root_two_pi

def normalize(values):
    centre = lax.optimization_barrier(jnp.mean(values, axis=-1, keepdims=True))
    centred = values - centre
    inv_dev = lax.rsqrt(lax.optimization_barrier(jnp.mean(centred * centred, axis=-1, keepdims=True)) + norm_eps)
    return (centred * inv_dev, inv_dev)

def normalize_back(grad_normed, normed, inv_dev):
    return inv_dev * (grad_normed - lax.optimization_barrier(jnp.mean(grad_normed, axis=-1, keepdims=True)) - normed * lax.optimization_barrier(jnp.mean(grad_normed * normed, axis=-1, keepdims=True)))

def product(form, left, right):
    return jnp.einsum(form, left.astype(jnp.float32), right.astype(jnp.float32))

def expand_rows(block_in, gain_conv, w_expand):
    flat_rows = block_in.reshape(-1, block_in.shape[-1]).astype(jnp.float32)
    normed, inv_dev = normalize(flat_rows)
    scaled = (normed * gain_conv).astype(jnp.bfloat16)
    pre_act = jnp.dot(scaled, w_expand, preferred_element_type=jnp.float32)
    return (normed, inv_dev, scaled, pre_act)

def depthwise(padded, w_depth, row_count, col_count):
    summed = jnp.zeros((row_count, col_count, padded.shape[-1]), jnp.float32)
    for row_off in range(3):
        for col_off in range(3):
            summed = summed + padded[row_off:row_off + row_count, col_off:col_off + col_count].astype(jnp.float32) * w_depth[row_off, col_off]
    return summed

def spread_back(grad_pad, w_depth, row_count, col_count):
    summed = jnp.zeros((row_count, col_count, grad_pad.shape[-1]), jnp.float32)
    for row_off in range(3):
        for col_off in range(3):
            summed = summed + grad_pad[2 - row_off:2 - row_off + row_count, 2 - col_off:2 - col_off + col_count].astype(jnp.float32) * w_depth[row_off, col_off]
    return summed

def depth_grad(hidden_pad, grad_conv, row_count, col_count):
    grad_wide = grad_conv.astype(jnp.float32)
    pieces = []
    for row_off in range(3):
        for col_off in range(3):
            pieces.append(lax.optimization_barrier(jnp.sum(hidden_pad[row_off:row_off + row_count, col_off:col_off + col_count].astype(jnp.float32) * grad_wide, axis=(0, 1))))
    return jnp.stack(pieces).reshape(3, 3, -1)

def window_back(windows, cot_windows, gain_attn, w_qkv, w_out):
    count, length, chans = windows.shape
    head_size = chans // HEADS
    scale_qk = head_size ** (-0.5)
    normed, inv_dev = normalize(windows.astype(jnp.float32))
    scaled = (normed * gain_attn).astype(jnp.bfloat16)
    projected = product('wtc,cd->wtd', scaled, w_qkv).astype(jnp.bfloat16)
    query = projected[..., :chans].reshape(count, length, HEADS, head_size)
    keys_all = projected[..., chans:2 * chans].reshape(count, length, HEADS, head_size)
    values_all = projected[..., 2 * chans:].reshape(count, length, HEADS, head_size)
    scores = product('wqhd,wkhd->whqk', query, keys_all) * scale_qk
    scores = scores - lax.optimization_barrier(jnp.max(scores, axis=-1, keepdims=True))
    expons = jnp.exp(scores)
    probs = expons / lax.optimization_barrier(jnp.sum(expons, axis=-1, keepdims=True))
    probs_b = probs.astype(jnp.bfloat16)
    attended = product('whqk,wkhd->wqhd', probs_b, values_all).astype(jnp.bfloat16).reshape(count, length, chans)
    grad_att = product('wtd,cd->wtc', cot_windows, w_out).astype(jnp.bfloat16).reshape(count, length, HEADS, head_size)
    grad_out = product('wtc,wtd->cd', attended, cot_windows)
    grad_probs = product('wqhd,wkhd->whqk', grad_att, values_all)
    grad_value = product('whqk,wqhd->wkhd', probs_b, grad_att).astype(jnp.bfloat16)
    grad_scores = (scale_qk * probs * (grad_probs - lax.optimization_barrier(jnp.sum(grad_probs * probs, axis=-1, keepdims=True)))).astype(jnp.bfloat16)
    grad_query = product('whqk,wkhd->wqhd', grad_scores, keys_all).astype(jnp.bfloat16)
    grad_key = product('whqk,wqhd->wkhd', grad_scores, query).astype(jnp.bfloat16)
    grad_proj = jnp.concatenate([grad_query.reshape(count, length, chans), grad_key.reshape(count, length, chans), grad_value.reshape(count, length, chans)], axis=-1)
    grad_qkv = product('wtc,wtd->cd', scaled, grad_proj)
    grad_scaled = product('wtd,cd->wtc', grad_proj, w_qkv)
    grad_gain = lax.optimization_barrier(jnp.sum(grad_scaled * normed, axis=(0, 1)))
    grad_branch = normalize_back(grad_scaled * gain_attn, normed, inv_dev).astype(jnp.bfloat16)
    return (grad_branch, (grad_qkv, grad_out, grad_gain))

def reference(field_in, cotangent, gain_conv, w_expand, w_depth, w_project, gain_attn, w_qkv, w_out):
    height, breadth, chans = field_in.shape
    expand_w = w_expand.shape[1]
    strip_len = 16
    strip_count = height // strip_len
    grad_scale = TOKENS ** (-0.5)
    padded_in = jnp.pad(field_in, ((2, 2), (0, 0), (0, 0)))

    def hidden_rows(start):
        rows_in = lax.dynamic_slice_in_dim(padded_in, start, strip_len + 4, 0)
        normed, inv_dev, scaled, pre_act = expand_rows(rows_in, gain_conv, w_expand)
        row_glob = start - 2 + jnp.arange(strip_len + 4, dtype=jnp.int32)
        inside = ((row_glob >= 0) & (row_glob < height)).astype(jnp.float32)
        hidden = (gelu_value(pre_act).reshape(strip_len + 4, breadth, expand_w) * inside[:, None, None]).astype(jnp.bfloat16)
        hidden_pad = jnp.pad(hidden, ((0, 0), (1, 1), (0, 0)))
        conv = depthwise(hidden_pad, w_depth, strip_len + 2, breadth)
        return (rows_in, normed, inv_dev, scaled, pre_act, hidden_pad, conv)

    def forward_strip(index):
        start = index.astype(jnp.int32) * strip_len
        rows_in, normed, inv_dev, scaled, pre_act, hidden_pad, conv = hidden_rows(start)
        acted = gelu_value(conv[1:strip_len + 1]).astype(jnp.bfloat16).reshape(-1, expand_w)
        core_in = rows_in[2:strip_len + 2].reshape(-1, chans).astype(jnp.float32)
        mixed = core_in + jnp.dot(acted, w_project, preferred_element_type=jnp.float32)
        return mixed.astype(jnp.bfloat16).reshape(strip_len, breadth, chans)
    mid_field = lax.map(forward_strip, jnp.arange(strip_count, dtype=jnp.int32)).reshape(height, breadth, chans)
    span_rows = height // GRID
    span_cols = breadth // GRID
    window_count = span_rows * span_cols
    group = 4 if window_count % 4 == 0 else 2 if window_count % 2 == 0 else 1

    def to_windows(values):
        arranged = values.reshape(GRID, span_rows, GRID, span_cols, chans).transpose(1, 3, 0, 2, 4)
        return arranged.reshape(window_count // group, group, GRID * GRID, chans)

    def attend_step(carry, window_pair):
        grad_branch, sums = window_back(window_pair[0], window_pair[1], gain_attn, w_qkv, w_out)
        return (tuple((before + added for before, added in zip(carry, sums))), grad_branch)
    attn_init = (jnp.zeros((chans, 3 * chans), jnp.float32), jnp.zeros((chans, chans), jnp.float32), jnp.zeros((chans,), jnp.float32))
    attn_sums, grad_windows = lax.scan(attend_step, attn_init, (to_windows(mid_field), to_windows(cotangent)))
    grad_branch = grad_windows.reshape(span_rows, span_cols, GRID, GRID, chans).transpose(2, 0, 3, 1, 4).reshape(height, breadth, chans)
    grad_mid = cotangent.astype(jnp.float32) + grad_branch.astype(jnp.float32)
    padded_grad = jnp.pad(grad_mid.astype(jnp.bfloat16), ((1, 1), (0, 0), (0, 0)))

    def back_strip(carry, index):
        start = index.astype(jnp.int32) * strip_len
        rows_in, normed, inv_dev, scaled, pre_act, hidden_pad, conv = hidden_rows(start)
        grad_rows = lax.dynamic_slice_in_dim(padded_grad, start, strip_len + 2, 0)
        acted = gelu_value(conv[1:strip_len + 1]).astype(jnp.bfloat16).reshape(-1, expand_w)
        grad_acted = jnp.dot(grad_rows.reshape(-1, chans), w_project.T, preferred_element_type=jnp.float32).astype(jnp.bfloat16)
        grad_conv = (grad_acted.astype(jnp.float32).reshape(conv.shape) * gelu_slope(conv)).astype(jnp.bfloat16)
        core_grad = grad_rows[1:strip_len + 1].reshape(-1, chans)
        grad_project = jnp.dot(acted.T, core_grad, preferred_element_type=jnp.float32)
        grad_conv_pad = jnp.pad(grad_conv, ((0, 0), (1, 1), (0, 0)))
        grad_hidden = spread_back(grad_conv_pad, w_depth, strip_len, breadth).reshape(-1, expand_w)
        grad_depth = depth_grad(hidden_pad[1:strip_len + 3], grad_conv[1:strip_len + 1], strip_len, breadth)
        core_pre = pre_act.reshape(strip_len + 4, breadth, expand_w)[2:strip_len + 2].reshape(-1, expand_w)
        grad_pre = (grad_hidden * gelu_slope(core_pre)).astype(jnp.bfloat16)
        core_scaled = scaled.reshape(strip_len + 4, breadth, chans)[2:strip_len + 2].reshape(-1, chans)
        core_normed = normed.reshape(strip_len + 4, breadth, chans)[2:strip_len + 2].reshape(-1, chans)
        core_inv = inv_dev.reshape(strip_len + 4, breadth, 1)[2:strip_len + 2].reshape(-1, 1)
        grad_expand = jnp.dot(core_scaled.T, grad_pre, preferred_element_type=jnp.float32)
        grad_scaled = jnp.dot(grad_pre, w_expand.T, preferred_element_type=jnp.float32)
        grad_gain = lax.optimization_barrier(jnp.sum(grad_scaled * core_normed, axis=0))
        core_mid = lax.dynamic_slice_in_dim(grad_mid, start, strip_len, 0).reshape(-1, chans)
        grad_rows_out = (core_mid + normalize_back(grad_scaled * gain_conv, core_normed, core_inv)).astype(jnp.bfloat16)
        sums = (grad_gain, grad_expand, grad_depth, grad_project)
        return (tuple((before + added for before, added in zip(carry, sums))), grad_rows_out.reshape(strip_len, breadth, chans))
    conv_init = (jnp.zeros((chans,), jnp.float32), jnp.zeros((chans, expand_w), jnp.float32), jnp.zeros((3, 3, expand_w), jnp.float32), jnp.zeros((expand_w, chans), jnp.float32))
    conv_sums, grad_strips = lax.scan(back_strip, conv_init, jnp.arange(strip_count, dtype=jnp.int32))
    grad_field = grad_strips.reshape(height, breadth, chans)
    return (grad_field, conv_sums[0] * grad_scale, conv_sums[1] * grad_scale, conv_sums[2] * grad_scale, conv_sums[3] * grad_scale, attn_sums[2] * grad_scale, attn_sums[0] * grad_scale, attn_sums[1] * grad_scale)
```

```python
import jax
import jax.numpy as jnp
from jax import lax
from jax.experimental import pallas as pl
from jax.experimental.pallas import tpu as pltpu
from jax.sharding import PartitionSpec as P

HEADS = 8
GRID = 16


norm_eps = 1e-05
root_half = 0.7071067811865476
inv_root_two_pi = 0.3989422804014327


F32 = jnp.float32
BF16 = jnp.bfloat16
EDGE = 8
BLOCK_E = 256
VMEM_BYTES = 56 * 1024 * 1024


def params():
    return pltpu.CompilerParams(
        dimension_semantics=("arbitrary",), vmem_limit_bytes=VMEM_BYTES
    )


def dot_nn(left, right):
    return lax.dot_general(left, right, (((1,), (0,)), ((), ())), preferred_element_type=F32)


def dot_nt(left, right):
    return lax.dot_general(left, right, (((1,), (1,)), ((), ())), preferred_element_type=F32)


def dot_tn(left, right):
    return lax.dot_general(left, right, (((0,), (0,)), ((), ())), preferred_element_type=F32)


def gelu_parts(values):
    half = 0.5 + 0.5 * lax.erf(values * root_half)
    slope = half + values * jnp.exp(-0.5 * values * values) * inv_root_two_pi
    return values * half, slope


def normalize(values, axis):
    centre = jnp.mean(values, axis=axis, keepdims=True)
    centred = values - centre
    inv_dev = lax.rsqrt(jnp.mean(centred * centred, axis=axis, keepdims=True) + norm_eps)
    return (centred * inv_dev, inv_dev)


def normalize_back(grad_normed, normed, inv_dev, axis):
    return inv_dev * (
        grad_normed
        - jnp.mean(grad_normed, axis=axis, keepdims=True)
        - normed * jnp.mean(grad_normed * normed, axis=axis, keepdims=True)
    )


def full(shape):
    return pl.BlockSpec(shape, lambda step: (0,) * len(shape))


def shift(axis, block, ahead):
    count = lax.axis_size(axis)
    forward = [(i, i + 1) for i in range(count - 1)]
    pairs = forward if ahead else [(target, source) for source, target in forward]
    return lax.ppermute(block, axis, pairs)


def halo(block):
    left = shift("col", block[:, -1:], True)
    right = shift("col", block[:, :1], False)
    wide_last = jnp.concatenate([left[-1:], block[-1:], right[-1:]], axis=1)
    wide_first = jnp.concatenate([left[:1], block[:1], right[:1]], axis=1)
    above = shift("row", wide_last, True)
    below = shift("row", wide_first, False)
    left = jnp.concatenate([above[:, :1], left, below[:, :1]], axis=0)
    right = jnp.concatenate([above[:, -1:], right, below[:, -1:]], axis=0)
    return above[:, 1:-1], below[:, 1:-1], left, right


def conv_forward(ext, core, gain, w_expand, w_taps, w_project, rows, cols):
    chans, expand_w = w_expand.shape
    cells = rows * cols
    around = cols + EDGE
    wide = cols + 2 * EDGE
    steps = expand_w // BLOCK_E

    def kernel(
        ext_ref, core_ref, gain_ref, we_ref, wd_ref, wp_ref,
        hid_out, act_out, sc_out, sp_out, mid_out,
        scaled_ref, pre_ref, hid_ref, acc_ref,
    ):
        step = pl.program_id(0)

        @pl.when(step == 0)
        def _():
            normed, _ = normalize(ext_ref[...].astype(F32), -1)
            scaled_ref[...] = (normed * gain_ref[...]).astype(BF16)
            acc_ref[...] = core_ref[...].astype(F32)

        pre_ref[...] = dot_nn(scaled_ref[...], we_ref[...])

        def put(row, value):
            tail = value[cols:]
            line = jnp.concatenate([tail, value[:cols], tail], axis=0)
            line = line.astype(BF16)
            hid_out[row] = line
            hid_ref[row] = line.astype(F32)

        for row in (0, rows + 1):
            edge = pre_ref[row * around : (row + 1) * around]
            put(row, edge * (0.5 + 0.5 * lax.erf(edge * root_half)))

        def expand_row(index, carry):
            pre = pre_ref[pl.ds(pl.multiple_of((index + 1) * around, 8), around)]
            value, slope = gelu_parts(pre)
            put(index + 1, value)
            sp_out[pl.ds(pl.multiple_of(index * cols, cols), cols)] = slope[:cols].astype(BF16)
            return carry

        lax.fori_loop(0, rows, expand_row, 0)

        def conv_row(index, carry):
            summed = None
            for p in range(3):
                for q in range(3):
                    tap = wd_ref[3 * p + q : 3 * p + q + 1]
                    term = hid_ref[index + p, EDGE - 1 + q : EDGE - 1 + q + cols] * tap
                    summed = term if summed is None else summed + term
            value, slope = gelu_parts(summed)
            here = pl.ds(pl.multiple_of(index * cols, cols), cols)
            act_out[here] = value.astype(BF16)
            sc_out[here] = slope.astype(BF16)
            return carry

        lax.fori_loop(0, rows, conv_row, 0)
        acc_ref[...] += dot_nn(act_out[...], wp_ref[...])

        @pl.when(step == steps - 1)
        def _():
            mid_out[...] = acc_ref[...].astype(BF16)

    ext_cells = (rows + 2) * around
    by_cell = pl.BlockSpec((cells, BLOCK_E), lambda step: (0, step))
    return pl.pallas_call(
        kernel,
        grid=(steps,),
        in_specs=[
            full((ext_cells, chans)),
            full((cells, chans)),
            full((1, chans)),
            pl.BlockSpec((chans, BLOCK_E), lambda step: (0, step)),
            pl.BlockSpec((9, BLOCK_E), lambda step: (0, step)),
            pl.BlockSpec((BLOCK_E, chans), lambda step: (step, 0)),
        ],
        out_specs=[
            pl.BlockSpec((rows + 2, wide, BLOCK_E), lambda step: (0, 0, step)),
            by_cell,
            by_cell,
            by_cell,
            full((cells, chans)),
        ],
        out_shape=[
            jax.ShapeDtypeStruct((rows + 2, wide, expand_w), BF16),
            jax.ShapeDtypeStruct((cells, expand_w), BF16),
            jax.ShapeDtypeStruct((cells, expand_w), BF16),
            jax.ShapeDtypeStruct((cells, expand_w), BF16),
            jax.ShapeDtypeStruct((cells, chans), BF16),
        ],
        scratch_shapes=[
            pltpu.VMEM((ext_cells, chans), BF16),
            pltpu.VMEM((ext_cells, BLOCK_E), F32),
            pltpu.VMEM((rows + 2, wide, BLOCK_E), F32),
            pltpu.VMEM((cells, chans), F32),
        ],
        compiler_params=params(),
        name="conv_forward",
    )(ext, core, gain, w_expand, w_taps, w_project)


def conv_grad(grad_mid_b, w_project, slope):
    cells, chans = grad_mid_b.shape
    expand_w = w_project.shape[0]

    def kernel(gm_ref, wp_ref, slope_ref, out_ref):
        grad_acted = dot_nt(gm_ref[...], wp_ref[...]).astype(BF16).astype(F32)
        out_ref[...] = (grad_acted * slope_ref[...].astype(F32)).astype(BF16)

    by_cell = pl.BlockSpec((cells, BLOCK_E), lambda step: (0, step))
    return pl.pallas_call(
        kernel,
        grid=(expand_w // BLOCK_E,),
        in_specs=[
            full((cells, chans)),
            pl.BlockSpec((BLOCK_E, chans), lambda step: (step, 0)),
            by_cell,
        ],
        out_specs=by_cell,
        out_shape=jax.ShapeDtypeStruct((cells, expand_w), BF16),
        compiler_params=params(),
        name="conv_grad",
    )(grad_mid_b, w_project, slope)


def conv_weight_grads(hidden, acted, grad_conv, grad_mid_t, rows, cols):
    cells, expand_w = acted.shape
    chans = grad_mid_t.shape[0]
    wide = hidden.shape[1]

    def kernel(hid_in, act_ref, gc_ref, gmt_ref, depth_out, proj_out, hid_ref):
        proj_out[...] = dot_nn(gmt_ref[...], act_ref[...])
        hid_ref[...] = hid_in[...].astype(F32)

        def one_row(index, carry):
            grad = gc_ref[pl.ds(pl.multiple_of(index * cols, cols), cols)].astype(F32)
            sums = []
            for p in range(3):
                for q in range(3):
                    term = hid_ref[index + p, EDGE - 1 + q : EDGE - 1 + q + cols] * grad
                    part = term[:8]
                    for low in range(8, cols, 8):
                        part = part + term[low : low + 8]
                    sums.append(carry[3 * p + q] + part)
            return tuple(sums)

        init = tuple(jnp.zeros((8, BLOCK_E), F32) for _ in range(9))
        sums = lax.fori_loop(0, rows, one_row, init)
        for tap in range(9):
            depth_out[tap : tap + 1] = jnp.sum(sums[tap], axis=0, keepdims=True)

    by_cell = pl.BlockSpec((cells, BLOCK_E), lambda step: (0, step))
    return pl.pallas_call(
        kernel,
        grid=(expand_w // BLOCK_E,),
        in_specs=[
            pl.BlockSpec((rows + 2, wide, BLOCK_E), lambda step: (0, 0, step)),
            by_cell,
            by_cell,
            full((chans, cells)),
        ],
        out_specs=[
            pl.BlockSpec((9, BLOCK_E), lambda step: (0, step)),
            pl.BlockSpec((chans, BLOCK_E), lambda step: (0, step)),
        ],
        out_shape=[
            jax.ShapeDtypeStruct((9, expand_w), F32),
            jax.ShapeDtypeStruct((chans, expand_w), F32),
        ],
        scratch_shapes=[pltpu.VMEM((rows + 2, wide, BLOCK_E), F32)],
        compiler_params=params(),
        cost_estimate=pl.CostEstimate(
            flops=2 * cells * expand_w * (chans + 9), bytes_accessed=32 << 20, transcendentals=0
        ),
        name="conv_weight_grads",
    )(hidden, acted, grad_conv, grad_mid_t)


def conv_back(grad_conv, line_pair, side_pair, slope, w_expand, w_taps, core, gain, grad_mid, rows, cols):
    cells, expand_w = grad_conv.shape
    chans = w_expand.shape[0]
    wide = cols + 2 * EDGE
    steps = expand_w // BLOCK_E

    def kernel(
        gc_ref, line_ref, side_ref, slope_ref, we_ref, wd_ref, core_ref, gain_ref, gm_ref,
        expand_out, gain_out, field_out,
        pad_ref, gpre_ref, scaled_t_ref, acc_ref,
    ):
        step = pl.program_id(0)

        @pl.when(step == 0)
        def _():
            normed, _ = normalize(core_ref[...].astype(F32), -1)
            scaled_t_ref[...] = (normed * gain_ref[...]).astype(BF16).T
            acc_ref[...] = jnp.zeros_like(acc_ref)

        def fill(index, carry):
            pad_ref[index + 1, EDGE : EDGE + cols] = gc_ref[
                pl.ds(pl.multiple_of(index * cols, cols), cols)
            ].astype(F32)
            return carry

        lax.fori_loop(0, rows, fill, 0)
        pad_ref[0, EDGE : EDGE + cols] = line_ref[0].astype(F32)
        pad_ref[rows + 1, EDGE : EDGE + cols] = line_ref[1].astype(F32)
        sides = side_ref[...].astype(F32)
        pad_ref[:, :EDGE] = sides[:, :EDGE]
        pad_ref[:, EDGE + cols :] = sides[:, EDGE:]

        def one_row(index, carry):
            summed = None
            for p in range(3):
                for q in range(3):
                    tap = wd_ref[3 * p + q : 3 * p + q + 1]
                    start = EDGE + 1 - q
                    term = pad_ref[index + 2 - p, start : start + cols] * tap
                    summed = term if summed is None else summed + term
            here = pl.ds(pl.multiple_of(index * cols, cols), cols)
            gpre_ref[here] = (summed * slope_ref[here].astype(F32)).astype(BF16)
            return carry

        lax.fori_loop(0, rows, one_row, 0)
        expand_out[...] = dot_nn(scaled_t_ref[...], gpre_ref[...])
        acc_ref[...] += dot_nt(gpre_ref[...], we_ref[...])

        @pl.when(step == steps - 1)
        def _():
            normed, inv_dev = normalize(core_ref[...].astype(F32), -1)
            grad_scaled = acc_ref[...]
            gain_out[...] = jnp.sum(grad_scaled * normed, axis=0, keepdims=True)
            back = normalize_back(grad_scaled * gain_ref[...], normed, inv_dev, -1)
            field_out[...] = (gm_ref[...] + back).astype(BF16)

    by_cell = pl.BlockSpec((cells, BLOCK_E), lambda step: (0, step))
    return pl.pallas_call(
        kernel,
        grid=(steps,),
        in_specs=[
            by_cell,
            pl.BlockSpec((2, cols, BLOCK_E), lambda step: (0, 0, step)),
            pl.BlockSpec((rows + 2, 2 * EDGE, BLOCK_E), lambda step: (0, 0, step)),
            by_cell,
            pl.BlockSpec((chans, BLOCK_E), lambda step: (0, step)),
            pl.BlockSpec((9, BLOCK_E), lambda step: (0, step)),
            full((cells, chans)),
            full((1, chans)),
            full((cells, chans)),
        ],
        out_specs=[
            pl.BlockSpec((chans, BLOCK_E), lambda step: (0, step)),
            full((1, chans)),
            full((cells, chans)),
        ],
        out_shape=[
            jax.ShapeDtypeStruct((chans, expand_w), F32),
            jax.ShapeDtypeStruct((1, chans), F32),
            jax.ShapeDtypeStruct((cells, chans), BF16),
        ],
        scratch_shapes=[
            pltpu.VMEM((rows + 2, wide, BLOCK_E), F32),
            pltpu.VMEM((cells, BLOCK_E), BF16),
            pltpu.VMEM((chans, cells), BF16),
            pltpu.VMEM((cells, chans), F32),
        ],
        compiler_params=params(),
        name="conv_back",
    )(grad_conv, line_pair, side_pair, slope, w_expand, w_taps, core, gain, grad_mid)


def grid_attention(mid_win, cot_win, gain_col, w_qkv, w_qkv_t, w_out):
    sources, windows, each, chans = mid_win.shape
    length = sources * each
    head = chans // HEADS
    scale = head ** (-0.5)

    def kernel(
        mid_ref, cot_ref, gain_ref, wq_ref, wqt_ref, wo_ref,
        branch_out, qkv_out, out_out, gain_out,
        proj_ref, gatt_ref, att_ref, gproj_ref, gg_ref,
    ):
        step = pl.program_id(0)

        @pl.when(step == 0)
        def _():
            qkv_out[...] = jnp.zeros_like(qkv_out)
            out_out[...] = jnp.zeros_like(out_out)
            gg_ref[...] = jnp.zeros_like(gg_ref)

        mid_t = mid_ref[...].astype(F32).reshape(length, chans).T
        cot = cot_ref[...].astype(F32).reshape(length, chans).astype(BF16)
        normed, inv_dev = normalize(mid_t, 0)
        gain = gain_ref[...]
        scaled = (normed * gain).astype(BF16)
        proj_ref[...] = dot_nn(wqt_ref[...], scaled).astype(BF16)
        gatt_ref[...] = dot_nt(wo_ref[...], cot).astype(BF16)
        for h in range(HEADS):
            at_q = slice(h * head, (h + 1) * head)
            at_k = slice(chans + h * head, chans + (h + 1) * head)
            at_v = slice(2 * chans + h * head, 2 * chans + (h + 1) * head)
            query, key, value = proj_ref[at_q], proj_ref[at_k], proj_ref[at_v]
            grad_att = gatt_ref[at_q]
            scores = dot_tn(key, query) * scale
            expons = jnp.exp(scores - jnp.max(scores, axis=0, keepdims=True))
            probs = expons * (1.0 / jnp.sum(expons, axis=0, keepdims=True))
            probs_b = probs.astype(BF16)
            att_ref[at_q] = dot_nn(value, probs_b).astype(BF16)
            gproj_ref[at_v] = dot_nt(grad_att, probs_b).astype(BF16)
            grad_probs = dot_tn(value, grad_att)
            row_sum = jnp.sum(grad_probs * probs, axis=0, keepdims=True)
            grad_scores = (scale * probs * (grad_probs - row_sum)).astype(BF16)
            gproj_ref[at_q] = dot_nn(key, grad_scores).astype(BF16)
            gproj_ref[at_k] = dot_nt(query, grad_scores).astype(BF16)
        out_out[...] += dot_nn(att_ref[...], cot)
        qkv_out[...] += dot_nt(gproj_ref[...], scaled)
        grad_scaled = dot_nn(wq_ref[...], gproj_ref[...])
        gg_ref[...] += grad_scaled * normed
        back = normalize_back(grad_scaled * gain, normed, inv_dev, 0)
        branch_out[...] = back.T.reshape(sources, 1, each, chans).astype(BF16)

        @pl.when(step == windows - 1)
        def _():
            gain_out[...] = jnp.sum(gg_ref[...], axis=1, keepdims=True)

    by_window = pl.BlockSpec((sources, 1, each, chans), lambda step: (0, step, 0, 0))
    return pl.pallas_call(
        kernel,
        grid=(windows,),
        in_specs=[
            by_window,
            by_window,
            full((chans, 1)),
            full((chans, 3 * chans)),
            full((3 * chans, chans)),
            full((chans, chans)),
        ],
        out_specs=[
            by_window,
            full((3 * chans, chans)),
            full((chans, chans)),
            full((chans, 1)),
        ],
        out_shape=[
            jax.ShapeDtypeStruct((sources, windows, each, chans), BF16),
            jax.ShapeDtypeStruct((3 * chans, chans), F32),
            jax.ShapeDtypeStruct((chans, chans), F32),
            jax.ShapeDtypeStruct((chans, 1), F32),
        ],
        scratch_shapes=[
            pltpu.VMEM((3 * chans, length), BF16),
            pltpu.VMEM((chans, length), BF16),
            pltpu.VMEM((chans, length), BF16),
            pltpu.VMEM((3 * chans, length), BF16),
            pltpu.VMEM((chans, length), F32),
        ],
        compiler_params=params(),
        name="grid_attention",
    )(mid_win, cot_win, gain_col, w_qkv, w_qkv_t, w_out)


def shards(field_in, cotangent, gain_conv, w_expand, w_depth, w_project, gain_attn, w_qkv, w_out):
    rows, cols, chans = field_in.shape
    expand_w = w_expand.shape[1]
    cells = rows * cols
    row_devices = lax.axis_size("row")
    col_devices = lax.axis_size("col")
    devices = row_devices * col_devices
    grad_scale = (cells * devices) ** (-0.5)
    per_row = GRID // row_devices
    per_col = GRID // col_devices
    part_rows = rows // per_row // row_devices
    part_cols = cols // per_col // col_devices

    def to_windows(tile):
        arranged = tile.reshape(
            per_row, row_devices, part_rows, per_col, col_devices, part_cols, chans
        )
        arranged = arranged.transpose(1, 4, 2, 5, 0, 3, 6).reshape(
            devices, part_rows * part_cols, per_row * per_col, chans
        )
        return lax.all_to_all(arranged, ("row", "col"), split_axis=0, concat_axis=0, tiled=True)

    cot_win = to_windows(cotangent)
    core = field_in.reshape(cells, chans)
    taps = w_depth.reshape(9, expand_w)
    above, below, left, right = halo(field_in)
    middle = jnp.concatenate([above, field_in, below], axis=0)
    gap = jnp.zeros((rows + 2, EDGE - 2, chans), BF16)
    ext = jnp.concatenate([middle, right, gap, left], axis=1).reshape(-1, chans)
    hidden, acted, slope_conv, slope_pre, mid = conv_forward(
        ext, core, gain_conv.reshape(1, chans), w_expand, taps, w_project, rows, cols
    )
    mid_win = to_windows(mid.reshape(rows, cols, chans))
    branch_win, grad_qkv_t, grad_out, grad_gain_attn = grid_attention(
        mid_win, cot_win, gain_attn.reshape(chans, 1), w_qkv, w_qkv.T, w_out
    )
    moved = lax.all_to_all(branch_win, ("row", "col"), split_axis=0, concat_axis=0, tiled=True)
    moved = moved.reshape(
        row_devices, col_devices, part_rows, part_cols, per_row, per_col, chans
    )
    branch = moved.transpose(4, 0, 2, 5, 1, 3, 6).reshape(cells, chans)
    grad_mid = cotangent.reshape(cells, chans).astype(F32) + branch.astype(F32)
    grad_mid_b = grad_mid.astype(BF16)
    grad_conv = conv_grad(grad_mid_b, w_project, slope_conv)
    above, below, left, right = halo(grad_conv.reshape(rows, cols, expand_w))
    grad_depth, grad_project_t = conv_weight_grads(
        hidden, acted, grad_conv, grad_mid_b.T, rows, cols
    )
    line_pair = jnp.concatenate([above, below], axis=0)
    gap = jnp.zeros((rows + 2, EDGE - 1, expand_w), BF16)
    side_pair = jnp.concatenate([gap, left, right, gap], axis=1)
    grad_expand, grad_gain_conv, grad_field = conv_back(
        grad_conv, line_pair, side_pair, slope_pre, w_expand, taps, core,
        gain_conv.reshape(1, chans), grad_mid, rows, cols,
    )
    sums = sum_over_devices(
        grad_expand, grad_project_t, grad_qkv_t, grad_out, grad_depth,
        grad_gain_conv, grad_gain_attn.reshape(1, chans),
    )
    grad_expand, grad_project_t, grad_qkv_t, grad_out, grad_depth, gain_c, gain_a = [
        value * grad_scale for value in sums
    ]
    return (
        grad_field.reshape(rows, cols, chans),
        gain_c.reshape(chans),
        grad_expand,
        grad_depth.reshape(3, 3, expand_w),
        grad_project_t.T,
        gain_a.reshape(chans),
        grad_qkv_t.T,
        grad_out,
    )


def sum_over_devices(*parts):
    large = [part.astype(BF16) for part in parts[:4]]
    small = parts[4:]
    return [
        value.astype(F32) for value in lax.psum(large, ("row", "col"))
    ] + list(lax.psum(small, ("row", "col")))


def solution(mesh):
    in_specs = (P("row", "col", None), P("row", "col", None), P(), P(), P(), P(), P(), P(), P())
    out_specs = (P("row", "col", None), P(), P(), P(), P(), P(), P(), P())
    return jax.shard_map(shards, mesh=mesh, in_specs=in_specs, out_specs=out_specs, check_vma=False)
```

```python
import jax
import jax.numpy as jnp
from jax import lax
from jax.experimental import pallas as pl
from jax.experimental.pallas import tpu as pltpu
from jax.sharding import PartitionSpec as P

HEADS = 8
GRID = 16


norm_eps = 1e-05
root_half = 0.7071067811865476
inv_root_two_pi = 0.3989422804014327


F32 = jnp.float32
BF16 = jnp.bfloat16
EDGE = 8
BLOCK_E = 256
VMEM_BYTES = 56 * 1024 * 1024


def params():
    return pltpu.CompilerParams(
        dimension_semantics=("arbitrary",), vmem_limit_bytes=VMEM_BYTES
    )


def dot_nn(left, right):
    return lax.dot_general(left, right, (((1,), (0,)), ((), ())), preferred_element_type=F32)


def dot_nt(left, right):
    return lax.dot_general(left, right, (((1,), (1,)), ((), ())), preferred_element_type=F32)


def dot_tn(left, right):
    return lax.dot_general(left, right, (((0,), (0,)), ((), ())), preferred_element_type=F32)


def gelu_parts(values):
    half = 0.5 + 0.5 * lax.erf(values * root_half)
    slope = half + values * jnp.exp(-0.5 * values * values) * inv_root_two_pi
    return values * half, slope


def normalize(values, axis):
    centre = jnp.mean(values, axis=axis, keepdims=True)
    centred = values - centre
    inv_dev = lax.rsqrt(jnp.mean(centred * centred, axis=axis, keepdims=True) + norm_eps)
    return (centred * inv_dev, inv_dev)


def normalize_back(grad_normed, normed, inv_dev, axis):
    return inv_dev * (
        grad_normed
        - jnp.mean(grad_normed, axis=axis, keepdims=True)
        - normed * jnp.mean(grad_normed * normed, axis=axis, keepdims=True)
    )


def full(shape):
    return pl.BlockSpec(shape, lambda step: (0,) * len(shape))


def shift(axis, block, ahead):
    count = lax.axis_size(axis)
    forward = [(i, i + 1) for i in range(count - 1)]
    pairs = forward if ahead else [(target, source) for source, target in forward]
    return lax.ppermute(block, axis, pairs)


def halo(block):
    left = shift("col", block[:, -1:], True)
    right = shift("col", block[:, :1], False)
    wide_last = jnp.concatenate([left[-1:], block[-1:], right[-1:]], axis=1)
    wide_first = jnp.concatenate([left[:1], block[:1], right[:1]], axis=1)
    above = shift("row", wide_last, True)
    below = shift("row", wide_first, False)
    left = jnp.concatenate([above[:, :1], left, below[:, :1]], axis=0)
    right = jnp.concatenate([above[:, -1:], right, below[:, -1:]], axis=0)
    return above[:, 1:-1], below[:, 1:-1], left, right


def conv_forward(ext, core, gain, w_expand, w_taps, w_project, rows, cols):
    chans, expand_w = w_expand.shape
    cells = rows * cols
    around = cols + EDGE
    wide = cols + 2 * EDGE
    steps = expand_w // BLOCK_E

    def kernel(
        ext_ref, core_ref, gain_ref, we_ref, wd_ref, wp_ref,
        hid_out, act_out, sc_out, sp_out, mid_out,
        scaled_ref, pre_ref, hid_ref, acc_ref,
    ):
        step = pl.program_id(0)

        @pl.when(step == 0)
        def _():
            normed, _ = normalize(ext_ref[...].astype(F32), -1)
            scaled_ref[...] = (normed * gain_ref[...]).astype(BF16)
            acc_ref[...] = core_ref[...].astype(F32)

        pre_ref[...] = dot_nn(scaled_ref[...], we_ref[...])

        def put(row, value):
            tail = value[cols:]
            line = jnp.concatenate([tail, value[:cols], tail], axis=0)
            line = line.astype(BF16)
            hid_out[row] = line
            hid_ref[row] = line.astype(F32)

        for row in (0, rows + 1):
            edge = pre_ref[row * around : (row + 1) * around]
            put(row, edge * (0.5 + 0.5 * lax.erf(edge * root_half)))

        def expand_row(index, carry):
            pre = pre_ref[pl.ds(pl.multiple_of((index + 1) * around, 8), around)]
            value, slope = gelu_parts(pre)
            put(index + 1, value)
            sp_out[pl.ds(pl.multiple_of(index * cols, cols), cols)] = slope[:cols].astype(BF16)
            return carry

        lax.fori_loop(0, rows, expand_row, 0)

        def conv_row(index, carry):
            summed = None
            for p in range(3):
                for q in range(3):
                    tap = wd_ref[3 * p + q : 3 * p + q + 1]
                    term = hid_ref[index + p, EDGE - 1 + q : EDGE - 1 + q + cols] * tap
                    summed = term if summed is None else summed + term
            value, slope = gelu_parts(summed)
            here = pl.ds(pl.multiple_of(index * cols, cols), cols)
            act_out[here] = value.astype(BF16)
            sc_out[here] = slope.astype(BF16)
            return carry

        lax.fori_loop(0, rows, conv_row, 0)
        acc_ref[...] += dot_nn(act_out[...], wp_ref[...])

        @pl.when(step == steps - 1)
        def _():
            mid_out[...] = acc_ref[...].astype(BF16)

    ext_cells = (rows + 2) * around
    by_cell = pl.BlockSpec((cells, BLOCK_E), lambda step: (0, step))
    return pl.pallas_call(
        kernel,
        grid=(steps,),
        in_specs=[
            full((ext_cells, chans)),
            full((cells, chans)),
            full((1, chans)),
            pl.BlockSpec((chans, BLOCK_E), lambda step: (0, step)),
            pl.BlockSpec((9, BLOCK_E), lambda step: (0, step)),
            pl.BlockSpec((BLOCK_E, chans), lambda step: (step, 0)),
        ],
        out_specs=[
            pl.BlockSpec((rows + 2, wide, BLOCK_E), lambda step: (0, 0, step)),
            by_cell,
            by_cell,
            by_cell,
            full((cells, chans)),
        ],
        out_shape=[
            jax.ShapeDtypeStruct((rows + 2, wide, expand_w), BF16),
            jax.ShapeDtypeStruct((cells, expand_w), BF16),
            jax.ShapeDtypeStruct((cells, expand_w), BF16),
            jax.ShapeDtypeStruct((cells, expand_w), BF16),
            jax.ShapeDtypeStruct((cells, chans), BF16),
        ],
        scratch_shapes=[
            pltpu.VMEM((ext_cells, chans), BF16),
            pltpu.VMEM((ext_cells, BLOCK_E), F32),
            pltpu.VMEM((rows + 2, wide, BLOCK_E), F32),
            pltpu.VMEM((cells, chans), F32),
        ],
        compiler_params=params(),
        name="conv_forward",
    )(ext, core, gain, w_expand, w_taps, w_project)


def conv_grad(grad_mid_b, w_project, slope):
    cells, chans = grad_mid_b.shape
    expand_w = w_project.shape[0]

    def kernel(gm_ref, wp_ref, slope_ref, out_ref):
        grad_acted = dot_nt(gm_ref[...], wp_ref[...]).astype(BF16).astype(F32)
        out_ref[...] = (grad_acted * slope_ref[...].astype(F32)).astype(BF16)

    by_cell = pl.BlockSpec((cells, BLOCK_E), lambda step: (0, step))
    return pl.pallas_call(
        kernel,
        grid=(expand_w // BLOCK_E,),
        in_specs=[
            full((cells, chans)),
            pl.BlockSpec((BLOCK_E, chans), lambda step: (step, 0)),
            by_cell,
        ],
        out_specs=by_cell,
        out_shape=jax.ShapeDtypeStruct((cells, expand_w), BF16),
        compiler_params=params(),
        name="conv_grad",
    )(grad_mid_b, w_project, slope)


def conv_weight_grads(hidden, acted, grad_conv, grad_mid_t, rows, cols):
    cells, expand_w = acted.shape
    chans = grad_mid_t.shape[0]
    wide = hidden.shape[1]

    def kernel(hid_in, act_ref, gc_ref, gmt_ref, depth_out, proj_out, hid_ref):
        proj_out[...] = dot_nn(gmt_ref[...], act_ref[...])
        hid_ref[...] = hid_in[...].astype(F32)

        def one_row(index, carry):
            grad = gc_ref[pl.ds(pl.multiple_of(index * cols, cols), cols)].astype(F32)
            sums = []
            for p in range(3):
                for q in range(3):
                    term = hid_ref[index + p, EDGE - 1 + q : EDGE - 1 + q + cols] * grad
                    part = term[:8]
                    for low in range(8, cols, 8):
                        part = part + term[low : low + 8]
                    sums.append(carry[3 * p + q] + part)
            return tuple(sums)

        init = tuple(jnp.zeros((8, BLOCK_E), F32) for _ in range(9))
        sums = lax.fori_loop(0, rows, one_row, init)
        for tap in range(9):
            depth_out[tap : tap + 1] = jnp.sum(sums[tap], axis=0, keepdims=True)

    by_cell = pl.BlockSpec((cells, BLOCK_E), lambda step: (0, step))
    return pl.pallas_call(
        kernel,
        grid=(expand_w // BLOCK_E,),
        in_specs=[
            pl.BlockSpec((rows + 2, wide, BLOCK_E), lambda step: (0, 0, step)),
            by_cell,
            by_cell,
            full((chans, cells)),
        ],
        out_specs=[
            pl.BlockSpec((9, BLOCK_E), lambda step: (0, step)),
            pl.BlockSpec((chans, BLOCK_E), lambda step: (step, 0)),
        ],
        out_shape=[
            jax.ShapeDtypeStruct((9, expand_w), F32),
            jax.ShapeDtypeStruct((expand_w // BLOCK_E * chans, BLOCK_E), F32),
        ],
        scratch_shapes=[pltpu.VMEM((rows + 2, wide, BLOCK_E), F32)],
        compiler_params=params(),
        cost_estimate=pl.CostEstimate(
            flops=2 * cells * expand_w * (chans + 9), bytes_accessed=32 << 20, transcendentals=0
        ),
        name="conv_weight_grads",
    )(hidden, acted, grad_conv, grad_mid_t)


def conv_back(grad_conv, line_pair, side_pair, slope, w_expand, w_taps, core, gain, grad_mid, rows, cols):
    cells, expand_w = grad_conv.shape
    chans = w_expand.shape[0]
    wide = cols + 2 * EDGE
    steps = expand_w // BLOCK_E

    def kernel(
        gc_ref, line_ref, side_ref, slope_ref, we_ref, wd_ref, core_ref, gain_ref, gm_ref,
        expand_out, gain_out, field_out,
        pad_ref, gpre_ref, scaled_t_ref, acc_ref,
    ):
        step = pl.program_id(0)

        @pl.when(step == 0)
        def _():
            normed, _ = normalize(core_ref[...].astype(F32), -1)
            scaled_t_ref[...] = (normed * gain_ref[...]).astype(BF16).T
            acc_ref[...] = jnp.zeros_like(acc_ref)

        def fill(index, carry):
            pad_ref[index + 1, EDGE : EDGE + cols] = gc_ref[
                pl.ds(pl.multiple_of(index * cols, cols), cols)
            ].astype(F32)
            return carry

        lax.fori_loop(0, rows, fill, 0)
        pad_ref[0, EDGE : EDGE + cols] = line_ref[0].astype(F32)
        pad_ref[rows + 1, EDGE : EDGE + cols] = line_ref[1].astype(F32)
        sides = side_ref[...].astype(F32)
        pad_ref[:, :EDGE] = sides[:, :EDGE]
        pad_ref[:, EDGE + cols :] = sides[:, EDGE:]

        def one_row(index, carry):
            summed = None
            for p in range(3):
                for q in range(3):
                    tap = wd_ref[3 * p + q : 3 * p + q + 1]
                    start = EDGE + 1 - q
                    term = pad_ref[index + 2 - p, start : start + cols] * tap
                    summed = term if summed is None else summed + term
            here = pl.ds(pl.multiple_of(index * cols, cols), cols)
            gpre_ref[here] = (summed * slope_ref[here].astype(F32)).astype(BF16)
            return carry

        lax.fori_loop(0, rows, one_row, 0)
        expand_out[...] = dot_nn(scaled_t_ref[...], gpre_ref[...])
        acc_ref[...] += dot_nt(gpre_ref[...], we_ref[...])

        @pl.when(step == steps - 1)
        def _():
            normed, inv_dev = normalize(core_ref[...].astype(F32), -1)
            grad_scaled = acc_ref[...]
            gain_out[...] = jnp.sum(grad_scaled * normed, axis=0, keepdims=True)
            back = normalize_back(grad_scaled * gain_ref[...], normed, inv_dev, -1)
            field_out[...] = (gm_ref[...] + back).astype(BF16)

    by_cell = pl.BlockSpec((cells, BLOCK_E), lambda step: (0, step))
    return pl.pallas_call(
        kernel,
        grid=(steps,),
        in_specs=[
            by_cell,
            pl.BlockSpec((2, cols, BLOCK_E), lambda step: (0, 0, step)),
            pl.BlockSpec((rows + 2, 2 * EDGE, BLOCK_E), lambda step: (0, 0, step)),
            by_cell,
            pl.BlockSpec((chans, BLOCK_E), lambda step: (0, step)),
            pl.BlockSpec((9, BLOCK_E), lambda step: (0, step)),
            full((cells, chans)),
            full((1, chans)),
            full((cells, chans)),
        ],
        out_specs=[
            pl.BlockSpec((chans, BLOCK_E), lambda step: (step, 0)),
            full((1, chans)),
            full((cells, chans)),
        ],
        out_shape=[
            jax.ShapeDtypeStruct((steps * chans, BLOCK_E), F32),
            jax.ShapeDtypeStruct((1, chans), F32),
            jax.ShapeDtypeStruct((cells, chans), BF16),
        ],
        scratch_shapes=[
            pltpu.VMEM((rows + 2, wide, BLOCK_E), F32),
            pltpu.VMEM((cells, BLOCK_E), BF16),
            pltpu.VMEM((chans, cells), BF16),
            pltpu.VMEM((cells, chans), F32),
        ],
        compiler_params=params(),
        name="conv_back",
    )(grad_conv, line_pair, side_pair, slope, w_expand, w_taps, core, gain, grad_mid)


def grid_attention(mid_win, cot_win, gain_col, w_qkv, w_qkv_t, w_out):
    sources, windows, each, chans = mid_win.shape
    length = sources * each
    head = chans // HEADS
    scale = head ** (-0.5)

    def kernel(
        mid_ref, cot_ref, gain_ref, wq_ref, wqt_ref, wo_ref,
        branch_out, qkv_out, out_out, gain_out,
        proj_ref, gatt_ref, att_ref, gproj_ref, gg_ref,
    ):
        step = pl.program_id(0)

        @pl.when(step == 0)
        def _():
            qkv_out[...] = jnp.zeros_like(qkv_out)
            out_out[...] = jnp.zeros_like(out_out)
            gg_ref[...] = jnp.zeros_like(gg_ref)

        mid_t = mid_ref[...].astype(F32).reshape(length, chans).T
        cot = cot_ref[...].astype(F32).reshape(length, chans).astype(BF16)
        normed, inv_dev = normalize(mid_t, 0)
        gain = gain_ref[...]
        scaled = (normed * gain).astype(BF16)
        proj_ref[...] = dot_nn(wqt_ref[...], scaled).astype(BF16)
        gatt_ref[...] = dot_nt(wo_ref[...], cot).astype(BF16)
        for h in range(HEADS):
            at_q = slice(h * head, (h + 1) * head)
            at_k = slice(chans + h * head, chans + (h + 1) * head)
            at_v = slice(2 * chans + h * head, 2 * chans + (h + 1) * head)
            query, key, value = proj_ref[at_q], proj_ref[at_k], proj_ref[at_v]
            grad_att = gatt_ref[at_q]
            scores = dot_tn(key, query) * scale
            expons = jnp.exp(scores - jnp.max(scores, axis=0, keepdims=True))
            probs = expons * (1.0 / jnp.sum(expons, axis=0, keepdims=True))
            probs_b = probs.astype(BF16)
            att_ref[at_q] = dot_nn(value, probs_b).astype(BF16)
            gproj_ref[at_v] = dot_nt(grad_att, probs_b).astype(BF16)
            grad_probs = dot_tn(value, grad_att)
            row_sum = jnp.sum(grad_probs * probs, axis=0, keepdims=True)
            grad_scores = (scale * probs * (grad_probs - row_sum)).astype(BF16)
            gproj_ref[at_q] = dot_nn(key, grad_scores).astype(BF16)
            gproj_ref[at_k] = dot_nt(query, grad_scores).astype(BF16)
        out_out[...] += dot_nn(att_ref[...], cot)
        qkv_out[...] += dot_nt(gproj_ref[...], scaled)
        grad_scaled = dot_nn(wq_ref[...], gproj_ref[...])
        gg_ref[...] += grad_scaled * normed
        back = normalize_back(grad_scaled * gain, normed, inv_dev, 0)
        branch_out[...] = back.T.reshape(sources, 1, each, chans).astype(BF16)

        @pl.when(step == windows - 1)
        def _():
            gain_out[...] = jnp.sum(gg_ref[...], axis=1, keepdims=True)

    by_window = pl.BlockSpec((sources, 1, each, chans), lambda step: (0, step, 0, 0))
    return pl.pallas_call(
        kernel,
        grid=(windows,),
        in_specs=[
            by_window,
            by_window,
            full((chans, 1)),
            full((chans, 3 * chans)),
            full((3 * chans, chans)),
            full((chans, chans)),
        ],
        out_specs=[
            by_window,
            full((3 * chans, chans)),
            full((chans, chans)),
            full((chans, 1)),
        ],
        out_shape=[
            jax.ShapeDtypeStruct((sources, windows, each, chans), BF16),
            jax.ShapeDtypeStruct((3 * chans, chans), F32),
            jax.ShapeDtypeStruct((chans, chans), F32),
            jax.ShapeDtypeStruct((chans, 1), F32),
        ],
        scratch_shapes=[
            pltpu.VMEM((3 * chans, length), BF16),
            pltpu.VMEM((chans, length), BF16),
            pltpu.VMEM((chans, length), BF16),
            pltpu.VMEM((3 * chans, length), BF16),
            pltpu.VMEM((chans, length), F32),
        ],
        compiler_params=params(),
        name="grid_attention",
    )(mid_win, cot_win, gain_col, w_qkv, w_qkv_t, w_out)


def shards(field_in, cotangent, gain_conv, w_expand, w_depth, w_project, gain_attn, w_qkv, w_out):
    rows, cols, chans = field_in.shape
    expand_w = w_expand.shape[1]
    cells = rows * cols
    row_devices = lax.axis_size("row")
    col_devices = lax.axis_size("col")
    devices = row_devices * col_devices
    grad_scale = (cells * devices) ** (-0.5)
    per_row = GRID // row_devices
    per_col = GRID // col_devices
    part_rows = rows // per_row // row_devices
    part_cols = cols // per_col // col_devices

    def to_windows(tile):
        arranged = tile.reshape(
            per_row, row_devices, part_rows, per_col, col_devices, part_cols, chans
        )
        arranged = arranged.transpose(1, 4, 2, 5, 0, 3, 6).reshape(
            devices, part_rows * part_cols, per_row * per_col, chans
        )
        return lax.all_to_all(arranged, ("row", "col"), split_axis=0, concat_axis=0, tiled=True)

    core = field_in.reshape(cells, chans)
    taps = w_depth.reshape(9, expand_w)
    above, below, left, right = halo(field_in)
    middle = jnp.concatenate([above, field_in, below], axis=0)
    gap = jnp.zeros((rows + 2, EDGE - 2, chans), BF16)
    ext = jnp.concatenate([middle, right, gap, left], axis=1).reshape(-1, chans)
    held, ext = lax.optimization_barrier((cotangent, ext))
    cot_win = to_windows(held)
    hidden, acted, slope_conv, slope_pre, mid = conv_forward(
        ext, core, gain_conv.reshape(1, chans), w_expand, taps, w_project, rows, cols
    )
    mid_win = to_windows(mid.reshape(rows, cols, chans))
    branch_win, grad_qkv_t, grad_out, grad_gain_attn = grid_attention(
        mid_win, cot_win, gain_attn.reshape(chans, 1), w_qkv, w_qkv.T, w_out
    )
    moved = lax.all_to_all(branch_win, ("row", "col"), split_axis=0, concat_axis=0, tiled=True)
    moved = moved.reshape(
        row_devices, col_devices, part_rows, part_cols, per_row, per_col, chans
    )
    branch = moved.transpose(4, 0, 2, 5, 1, 3, 6).reshape(cells, chans)
    grad_mid = cotangent.reshape(cells, chans).astype(F32) + branch.astype(F32)
    grad_mid_b = grad_mid.astype(BF16)
    grad_conv = conv_grad(grad_mid_b, w_project, slope_conv)
    above, below, left, right = halo(grad_conv.reshape(rows, cols, expand_w))
    grad_depth, grad_project_t = conv_weight_grads(
        hidden, acted, grad_conv, grad_mid_b.T, rows, cols
    )
    line_pair = jnp.concatenate([above, below], axis=0)
    gap = jnp.zeros((rows + 2, EDGE - 1, expand_w), BF16)
    side_pair = jnp.concatenate([gap, left, right, gap], axis=1)
    grad_expand, grad_gain_conv, grad_field = conv_back(
        grad_conv, line_pair, side_pair, slope_pre, w_expand, taps, core,
        gain_conv.reshape(1, chans), grad_mid, rows, cols,
    )
    small_rows = 9 * expand_w // chans
    small = jnp.concatenate(
        [
            grad_depth.reshape(small_rows, chans),
            grad_gain_conv,
            grad_gain_attn.reshape(1, chans),
            jnp.zeros((-(small_rows + 2) % 8, chans), F32),
        ]
    )
    grad_expand, grad_project, grad_qkv, grad_out, small = sum_over_devices(
        grad_expand, grad_project_t, grad_qkv_t, grad_out, small, grad_scale
    )
    return (
        grad_field.reshape(rows, cols, chans),
        small[small_rows],
        grad_expand,
        small[:small_rows].reshape(3, 3, expand_w),
        grad_project,
        small[small_rows + 1],
        grad_qkv,
        grad_out,
    )


def sum_over_devices(expand, project_t, qkv_t, out, small, grad_scale):
    lanes = 128
    chans = out.shape[0]
    halves = out.shape[1] // lanes
    parts = (expand, project_t, qkv_t, out, small)
    starts = [0]
    for part in parts:
        starts.append(starts[-1] + part.shape[0])
    blocks = expand.shape[0] // chans
    sizes = {axis: lax.axis_size(axis) for axis in ("row", "col")}
    devices = sizes["row"] * sizes["col"]
    unit = 16 * devices
    total = -(-starts[-1] // unit) * unit
    row_bits = [("row", bit) for bit in range(sizes["row"].bit_length() - 1)]
    col_bits = [("col", bit) for bit in range(sizes["col"].bit_length() - 1)]
    orders = [row_bits + col_bits, row_bits[:1] + col_bits + row_bits[1:]]
    count = len(orders[0])

    def kernel(
        ex_ref, pr_ref, qk_ref, ou_ref, sm_ref,
        ex_out, pr_out, qk_out, ou_out, sm_out,
        acc_ref, send_ref, recv_ref, got_ref, send_sem, recv_sem,
    ):
        places = {"row": lax.axis_index("row"), "col": lax.axis_index("col")}

        def partner(axis, bit):
            mine = lax.rem(places[axis] // (1 << bit), 2)
            return mine, {axis: places[axis] + (1 - 2 * mine) * (1 << bit)}

        barrier = pltpu.get_barrier_semaphore()
        for axis, bit in orders[0]:
            _, target = partner(axis, bit)
            pl.semaphore_signal(
                barrier, inc=1, device_id=target, device_id_type=pl.DeviceIdType.MESH
            )
        pl.semaphore_wait(barrier, count)

        for lane in range(halves):
            span = slice(lane * lanes, (lane + 1) * lanes)
            for start, ref in zip(starts, (ex_ref, pr_ref, qk_ref, ou_ref, sm_ref)):
                acc_ref[lane, start : start + ref.shape[0]] = ref[:, span]
            if total > starts[-1]:
                acc_ref[lane, starts[-1] : total] = jnp.zeros((total - starts[-1], lanes), F32)

        offsets = [0] * halves

        def reduce_start(lane, step):
            size = total >> (step + 1)
            mine, target = partner(*orders[lane % 2][step])
            away = pl.multiple_of(offsets[lane] + (1 - mine) * size, 16)
            offsets[lane] = pl.multiple_of(offsets[lane] + mine * size, 16)
            send_ref[lane, pl.ds(away, size)] = acc_ref[lane, pl.ds(away, size)].astype(BF16)
            copy = pltpu.make_async_remote_copy(
                src_ref=send_ref.at[lane, pl.ds(away, size)],
                dst_ref=recv_ref.at[lane, pl.ds(total - 2 * size, size)],
                send_sem=send_sem.at[lane, step],
                recv_sem=recv_sem.at[lane, step],
                device_id=target,
                device_id_type=pl.DeviceIdType.MESH,
            )
            copy.start()
            return copy

        def reduce_end(lane, step, copy):
            size = total >> (step + 1)
            copy.wait()
            kept = pl.ds(offsets[lane], size)
            acc_ref[lane, kept] += recv_ref[lane, pl.ds(total - 2 * size, size)].astype(F32)

        copies = [reduce_start(lane, 0) for lane in range(halves)]
        for step in range(count):
            for lane in range(halves):
                reduce_end(lane, step, copies[lane])
                if step + 1 < count:
                    copies[lane] = reduce_start(lane, step + 1)

        def gather_start(lane, step):
            size = total >> (step + 1)
            mine, target = partner(*orders[lane % 2][step])
            own = pl.ds(offsets[lane], size)
            copy = pltpu.make_async_remote_copy(
                src_ref=got_ref.at[lane, own],
                dst_ref=got_ref.at[lane, own],
                send_sem=send_sem.at[lane, count + step],
                recv_sem=recv_sem.at[lane, count + step],
                device_id=target,
                device_id_type=pl.DeviceIdType.MESH,
            )
            copy.start()
            offsets[lane] = pl.multiple_of(offsets[lane] - mine * size, 16)
            return copy

        for lane in range(halves):
            own = pl.ds(offsets[lane], total >> count)
            got_ref[lane, own] = (acc_ref[lane, own] * grad_scale).astype(BF16)
            copies[lane] = gather_start(lane, count - 1)
        for step in reversed(range(count)):
            for lane in range(halves):
                copies[lane].wait()
                if step:
                    copies[lane] = gather_start(lane, step - 1)

        def read(start, size):
            return jnp.concatenate(
                [got_ref[lane, start : start + size].astype(F32) for lane in range(halves)], axis=1
            )

        for block in range(blocks):
            low, high = block * chans, (block + 1) * chans
            ex_out[:, low:high] = read(starts[0] + low, chans)
            pr_out[low:high] = read(starts[1] + low, chans).T
        for block in range(qkv_t.shape[0] // chans):
            low, high = block * chans, (block + 1) * chans
            qk_out[:, low:high] = read(starts[2] + low, chans).T
        ou_out[...] = read(starts[3], chans)
        packed = -(-small.shape[0] // 16) * 16
        sm_out[...] = read(starts[4], packed)[: small.shape[0]]

    whole = [pl.BlockSpec(memory_space=pltpu.VMEM)] * 5
    return pl.pallas_call(
        kernel,
        in_specs=whole,
        out_specs=whole,
        out_shape=[
            jax.ShapeDtypeStruct((chans, blocks * chans), F32),
            jax.ShapeDtypeStruct((blocks * chans, chans), F32),
            jax.ShapeDtypeStruct((chans, qkv_t.shape[0]), F32),
            jax.ShapeDtypeStruct(out.shape, F32),
            jax.ShapeDtypeStruct(small.shape, F32),
        ],
        scratch_shapes=[
            pltpu.VMEM((halves, total, lanes), F32),
            pltpu.VMEM((halves, total, lanes), BF16),
            pltpu.VMEM((halves, total, lanes), BF16),
            pltpu.VMEM((halves, total, lanes), BF16),
            pltpu.SemaphoreType.DMA((halves, 2 * count)),
            pltpu.SemaphoreType.DMA((halves, 2 * count)),
        ],
        compiler_params=pltpu.CompilerParams(
            collective_id=0, has_side_effects=True, vmem_limit_bytes=VMEM_BYTES
        ),
        name="sum_over_devices",
    )(*parts)


def solution(mesh):
    in_specs = (P("row", "col", None), P("row", "col", None), P(), P(), P(), P(), P(), P(), P())
    out_specs = (P("row", "col", None), P(), P(), P(), P(), P(), P(), P())
    return jax.shard_map(shards, mesh=mesh, in_specs=in_specs, out_specs=out_specs, check_vma=False)
```

```python
import jax
import jax.numpy as jnp
from jax import lax
from jax.experimental import pallas as pl
from jax.experimental.pallas import tpu as pltpu
from jax.sharding import PartitionSpec as P

HEADS = 8
GRID = 16


norm_eps = 1e-05
root_half = 0.7071067811865476
inv_root_two_pi = 0.3989422804014327


F32 = jnp.float32
BF16 = jnp.bfloat16
EDGE = 8
log2_e = 1.4426950408889634
BLOCK_E = 256
VMEM_BYTES = 56 * 1024 * 1024


def params():
    return pltpu.CompilerParams(
        dimension_semantics=("arbitrary",), vmem_limit_bytes=VMEM_BYTES
    )


def dot_nn(left, right):
    return lax.dot_general(left, right, (((1,), (0,)), ((), ())), preferred_element_type=F32)


def dot_nt(left, right):
    return lax.dot_general(left, right, (((1,), (1,)), ((), ())), preferred_element_type=F32)


def dot_tn(left, right):
    return lax.dot_general(left, right, (((0,), (0,)), ((), ())), preferred_element_type=F32)


def gelu_parts(values):
    half = 0.5 + 0.5 * lax.erf(values * root_half)
    slope = half + values * jnp.exp(-0.5 * values * values) * inv_root_two_pi
    return values * half, slope


def normalize(values, axis):
    centre = jnp.mean(values, axis=axis, keepdims=True)
    centred = values - centre
    inv_dev = lax.rsqrt(jnp.mean(centred * centred, axis=axis, keepdims=True) + norm_eps)
    return (centred * inv_dev, inv_dev)


def normalize_back(grad_normed, normed, inv_dev, axis):
    return inv_dev * (
        grad_normed
        - jnp.mean(grad_normed, axis=axis, keepdims=True)
        - normed * jnp.mean(grad_normed * normed, axis=axis, keepdims=True)
    )


def cost(micros):
    return pl.CostEstimate(flops=int(micros * 1.1e9), bytes_accessed=1 << 20, transcendentals=0)


def full(shape):
    return pl.BlockSpec(shape, lambda step: (0,) * len(shape))


def shift(axis, block, ahead):
    count = lax.axis_size(axis)
    forward = [(i, i + 1) for i in range(count - 1)]
    pairs = forward if ahead else [(target, source) for source, target in forward]
    return lax.ppermute(block, axis, pairs)


def halo(block):
    left = shift("col", block[:, -1:], True)
    right = shift("col", block[:, :1], False)
    wide_last = jnp.concatenate([left[-1:], block[-1:], right[-1:]], axis=1)
    wide_first = jnp.concatenate([left[:1], block[:1], right[:1]], axis=1)
    first = left
    above = shift("row", wide_last, True)
    below = shift("row", wide_first, False)
    left = jnp.concatenate([above[:, :1], left, below[:, :1]], axis=0)
    right = jnp.concatenate([above[:, -1:], right, below[:, -1:]], axis=0)
    return above[:, 1:-1], below[:, 1:-1], left, right, first


def conv_forward(ext, core, gain, w_expand, w_taps, w_project, rows, cols):
    chans, expand_w = w_expand.shape
    cells = rows * cols
    around = cols + EDGE
    wide = cols + 2 * EDGE
    steps = expand_w // BLOCK_E

    def kernel(
        ext_ref, core_ref, gain_ref, we_ref, wd_ref, wp_ref,
        hid_out, act_out, sc_out, sp_out, mid_out,
        scaled_ref, pre_ref, hid_ref, acc_ref,
    ):
        step = pl.program_id(0)

        @pl.when(step == 0)
        def _():
            normed, _ = normalize(ext_ref[...].astype(F32), -1)
            scaled_ref[...] = (normed * gain_ref[...]).astype(BF16)
            acc_ref[...] = core_ref[...].astype(F32)

        pre_ref[...] = dot_nn(scaled_ref[...], we_ref[...])

        def put(row, value):
            tail = value[cols:]
            line = jnp.concatenate([tail, value[:cols], tail], axis=0)
            line = line.astype(BF16)
            hid_out[row] = line
            hid_ref[row] = line.astype(F32)

        for row in (0, rows + 1):
            edge = pre_ref[row * around : (row + 1) * around]
            put(row, edge * (0.5 + 0.5 * lax.erf(edge * root_half)))

        def expand_row(index, carry):
            pre = pre_ref[pl.ds(pl.multiple_of((index + 1) * around, 8), around)]
            value, slope = gelu_parts(pre)
            put(index + 1, value)
            sp_out[pl.ds(pl.multiple_of(index * cols, cols), cols)] = slope[:cols].astype(BF16)
            return carry

        lax.fori_loop(0, rows, expand_row, 0)

        def conv_row(index, carry):
            summed = None
            for p in range(3):
                for q in range(3):
                    tap = wd_ref[3 * p + q : 3 * p + q + 1]
                    term = hid_ref[index + p, EDGE - 1 + q : EDGE - 1 + q + cols] * tap
                    summed = term if summed is None else summed + term
            value, slope = gelu_parts(summed)
            here = pl.ds(pl.multiple_of(index * cols, cols), cols)
            act_out[here] = value.astype(BF16)
            sc_out[here] = slope.astype(BF16)
            return carry

        lax.fori_loop(0, rows, conv_row, 0)
        acc_ref[...] += dot_nn(act_out[...], wp_ref[...])

        @pl.when(step == steps - 1)
        def _():
            mid_out[...] = acc_ref[...].astype(BF16)

    ext_cells = (rows + 2) * around
    by_cell = pl.BlockSpec((cells, BLOCK_E), lambda step: (0, step))
    return pl.pallas_call(
        kernel,
        grid=(steps,),
        in_specs=[
            full((ext_cells, chans)),
            full((cells, chans)),
            full((1, chans)),
            pl.BlockSpec((chans, BLOCK_E), lambda step: (0, step)),
            pl.BlockSpec((9, BLOCK_E), lambda step: (0, step)),
            pl.BlockSpec((BLOCK_E, chans), lambda step: (step, 0)),
        ],
        out_specs=[
            pl.BlockSpec((rows + 2, wide, BLOCK_E), lambda step: (0, 0, step)),
            by_cell,
            by_cell,
            by_cell,
            full((cells, chans)),
        ],
        out_shape=[
            jax.ShapeDtypeStruct((rows + 2, wide, expand_w), BF16),
            jax.ShapeDtypeStruct((cells, expand_w), BF16),
            jax.ShapeDtypeStruct((cells, expand_w), BF16),
            jax.ShapeDtypeStruct((cells, expand_w), BF16),
            jax.ShapeDtypeStruct((cells, chans), BF16),
        ],
        scratch_shapes=[
            pltpu.VMEM((ext_cells, chans), BF16),
            pltpu.VMEM((ext_cells, BLOCK_E), F32),
            pltpu.VMEM((rows + 2, wide, BLOCK_E), F32),
            pltpu.VMEM((cells, chans), F32),
        ],
        compiler_params=params(),
        cost_estimate=cost(34),
        name="conv_forward",
    )(ext, core, gain, w_expand, w_taps, w_project)


def conv_grad(cotangent, branch, w_project, slope):
    cells, chans = cotangent.shape
    expand_w = w_project.shape[0]

    def kernel(cot_ref, branch_ref, wp_ref, slope_ref, out_ref, mid_out, mid_t_out, gm_ref):
        @pl.when(pl.program_id(0) == 0)
        def _():
            grad_mid = cot_ref[...].astype(F32) + branch_ref[...].astype(F32)
            mid_out[...] = grad_mid
            rounded = grad_mid.astype(BF16)
            gm_ref[...] = rounded
            mid_t_out[...] = rounded.T

        grad_acted = dot_nt(gm_ref[...], wp_ref[...]).astype(BF16).astype(F32)
        out_ref[...] = (grad_acted * slope_ref[...].astype(F32)).astype(BF16)

    by_cell = pl.BlockSpec((cells, BLOCK_E), lambda step: (0, step))
    return pl.pallas_call(
        kernel,
        grid=(expand_w // BLOCK_E,),
        in_specs=[
            full((cells, chans)),
            full((cells, chans)),
            pl.BlockSpec((BLOCK_E, chans), lambda step: (step, 0)),
            by_cell,
        ],
        out_specs=[by_cell, full((cells, chans)), full((chans, cells))],
        out_shape=[
            jax.ShapeDtypeStruct((cells, expand_w), BF16),
            jax.ShapeDtypeStruct((cells, chans), F32),
            jax.ShapeDtypeStruct((chans, cells), BF16),
        ],
        scratch_shapes=[pltpu.VMEM((cells, chans), BF16)],
        compiler_params=params(),
        cost_estimate=cost(8),
        name="conv_grad",
    )(cotangent, branch, w_project, slope)


def project_grad(acted, grad_mid_t):
    cells, expand_w = acted.shape
    chans = grad_mid_t.shape[0]

    def kernel(act_ref, gmt_ref, proj_out):
        proj_out[...] = dot_nn(gmt_ref[...], act_ref[...])

    return pl.pallas_call(
        kernel,
        grid=(expand_w // BLOCK_E,),
        in_specs=[
            pl.BlockSpec((cells, BLOCK_E), lambda step: (0, step)),
            full((chans, cells)),
        ],
        out_specs=pl.BlockSpec((chans, BLOCK_E), lambda step: (step, 0)),
        out_shape=jax.ShapeDtypeStruct((expand_w // BLOCK_E * chans, BLOCK_E), F32),
        compiler_params=params(),
        cost_estimate=cost(4),
        name="project_grad",
    )(acted, grad_mid_t)


def depth_grad(hidden, grad_conv, rows, cols):
    cells, expand_w = grad_conv.shape
    wide = hidden.shape[1]

    def kernel(hid_in, gc_ref, depth_out, hid_ref):
        hid_ref[...] = hid_in[...].astype(F32)

        def one_row(index, carry):
            grad = gc_ref[pl.ds(pl.multiple_of(index * cols, cols), cols)].astype(F32)
            sums = []
            for p in range(3):
                for q in range(3):
                    term = hid_ref[index + p, EDGE - 1 + q : EDGE - 1 + q + cols] * grad
                    part = term[:8]
                    for low in range(8, cols, 8):
                        part = part + term[low : low + 8]
                    sums.append(carry[3 * p + q] + part)
            return tuple(sums)

        init = tuple(jnp.zeros((8, BLOCK_E), F32) for _ in range(9))
        sums = lax.fori_loop(0, rows, one_row, init)
        for tap in range(9):
            depth_out[tap : tap + 1] = jnp.sum(sums[tap], axis=0, keepdims=True)

    by_cell = pl.BlockSpec((cells, BLOCK_E), lambda step: (0, step))
    return pl.pallas_call(
        kernel,
        grid=(expand_w // BLOCK_E,),
        in_specs=[
            pl.BlockSpec((rows + 2, wide, BLOCK_E), lambda step: (0, 0, step)),
            by_cell,
        ],
        out_specs=pl.BlockSpec((9, BLOCK_E), lambda step: (0, step)),
        out_shape=jax.ShapeDtypeStruct((9, expand_w), F32),
        scratch_shapes=[pltpu.VMEM((rows + 2, wide, BLOCK_E), F32)],
        compiler_params=params(),
        cost_estimate=cost(12),
        name="depth_grad",
    )(hidden, grad_conv)


def conv_back(grad_conv, line_pair, side_pair, slope, w_expand, w_taps, core, gain, grad_mid, rows, cols):
    cells, expand_w = grad_conv.shape
    chans = w_expand.shape[0]
    wide = cols + 2 * EDGE
    steps = expand_w // BLOCK_E

    def kernel(
        gc_ref, line_ref, side_ref, slope_ref, we_ref, wd_ref, core_ref, gain_ref, gm_ref,
        expand_out, gain_out, field_out,
        pad_ref, gpre_ref, scaled_t_ref, acc_ref,
    ):
        step = pl.program_id(0)

        @pl.when(step == 0)
        def _():
            normed, _ = normalize(core_ref[...].astype(F32), -1)
            scaled_t_ref[...] = (normed * gain_ref[...]).astype(BF16).T
            acc_ref[...] = jnp.zeros_like(acc_ref)

        def fill(index, carry):
            pad_ref[index + 1, EDGE : EDGE + cols] = gc_ref[
                pl.ds(pl.multiple_of(index * cols, cols), cols)
            ].astype(F32)
            return carry

        lax.fori_loop(0, rows, fill, 0)
        pad_ref[0, EDGE : EDGE + cols] = line_ref[0].astype(F32)
        pad_ref[rows + 1, EDGE : EDGE + cols] = line_ref[1].astype(F32)
        sides = side_ref[...].astype(F32)
        pad_ref[:, :EDGE] = sides[:, :EDGE]
        pad_ref[:, EDGE + cols :] = sides[:, EDGE:]

        def one_row(index, carry):
            summed = None
            for p in range(3):
                for q in range(3):
                    tap = wd_ref[3 * p + q : 3 * p + q + 1]
                    start = EDGE + 1 - q
                    term = pad_ref[index + 2 - p, start : start + cols] * tap
                    summed = term if summed is None else summed + term
            here = pl.ds(pl.multiple_of(index * cols, cols), cols)
            gpre_ref[here] = (summed * slope_ref[here].astype(F32)).astype(BF16)
            return carry

        lax.fori_loop(0, rows, one_row, 0)
        expand_out[...] = dot_nn(scaled_t_ref[...], gpre_ref[...])
        acc_ref[...] += dot_nt(gpre_ref[...], we_ref[...])

        @pl.when(step == steps - 1)
        def _():
            normed, inv_dev = normalize(core_ref[...].astype(F32), -1)
            grad_scaled = acc_ref[...]
            gain_out[...] = jnp.sum(grad_scaled * normed, axis=0, keepdims=True)
            back = normalize_back(grad_scaled * gain_ref[...], normed, inv_dev, -1)
            field_out[...] = (gm_ref[...] + back).astype(BF16)

    by_cell = pl.BlockSpec((cells, BLOCK_E), lambda step: (0, step))
    return pl.pallas_call(
        kernel,
        grid=(steps,),
        in_specs=[
            by_cell,
            pl.BlockSpec((2, cols, BLOCK_E), lambda step: (0, 0, step)),
            pl.BlockSpec((rows + 2, 2 * EDGE, BLOCK_E), lambda step: (0, 0, step)),
            by_cell,
            pl.BlockSpec((chans, BLOCK_E), lambda step: (0, step)),
            pl.BlockSpec((9, BLOCK_E), lambda step: (0, step)),
            full((cells, chans)),
            full((1, chans)),
            full((cells, chans)),
        ],
        out_specs=[
            pl.BlockSpec((chans, BLOCK_E), lambda step: (step, 0)),
            full((1, chans)),
            full((cells, chans)),
        ],
        out_shape=[
            jax.ShapeDtypeStruct((steps * chans, BLOCK_E), F32),
            jax.ShapeDtypeStruct((1, chans), F32),
            jax.ShapeDtypeStruct((cells, chans), BF16),
        ],
        scratch_shapes=[
            pltpu.VMEM((rows + 2, wide, BLOCK_E), F32),
            pltpu.VMEM((cells, BLOCK_E), BF16),
            pltpu.VMEM((chans, cells), BF16),
            pltpu.VMEM((cells, chans), F32),
        ],
        compiler_params=params(),
        cost_estimate=cost(24),
        name="conv_back",
    )(grad_conv, line_pair, side_pair, slope, w_expand, w_taps, core, gain, grad_mid)


def grid_attention(mid_win, cot_win, gain_col, w_qkv, w_qkv_t, w_out):
    sources, windows, each, chans = mid_win.shape
    length = sources * each
    head = chans // HEADS
    scale = head ** (-0.5)

    def kernel(
        mid_ref, cot_ref, gain_ref, wq_ref, wqt_ref, wo_ref,
        branch_out, qkv_out, out_out, gain_out,
        proj_ref, gatt_ref, att_ref, gproj_ref, gg_ref,
    ):
        step = pl.program_id(0)

        @pl.when(step == 0)
        def _():
            qkv_out[...] = jnp.zeros_like(qkv_out)
            out_out[...] = jnp.zeros_like(out_out)
            gg_ref[...] = jnp.zeros_like(gg_ref)

        mid_t = mid_ref[...].astype(F32).reshape(length, chans).T
        cot = cot_ref[...].astype(F32).reshape(length, chans).astype(BF16)
        normed, inv_dev = normalize(mid_t, 0)
        gain = gain_ref[...]
        scaled = (normed * gain).astype(BF16)
        proj_ref[...] = dot_nn(wqt_ref[...], scaled).astype(BF16)
        gatt_ref[...] = dot_nt(wo_ref[...], cot).astype(BF16)
        for h in range(HEADS):
            at_q = slice(h * head, (h + 1) * head)
            at_k = slice(chans + h * head, chans + (h + 1) * head)
            at_v = slice(2 * chans + h * head, 2 * chans + (h + 1) * head)
            query, key, value = proj_ref[at_q], proj_ref[at_k], proj_ref[at_v]
            grad_att = gatt_ref[at_q]
            scores = dot_tn(key, query)
            expons = jnp.exp2((scores - jnp.max(scores, axis=0, keepdims=True)) * (scale * log2_e))
            probs = expons * (1.0 / jnp.sum(expons, axis=0, keepdims=True))
            probs_b = probs.astype(BF16)
            att_ref[at_q] = dot_nn(value, probs_b).astype(BF16)
            gproj_ref[at_v] = dot_nt(grad_att, probs_b).astype(BF16)
            grad_probs = dot_tn(value, grad_att)
            row_sum = jnp.sum(grad_probs * probs, axis=0, keepdims=True)
            grad_scores = (probs * (grad_probs - row_sum)).astype(BF16)
            gproj_ref[at_q] = (scale * dot_nn(key, grad_scores)).astype(BF16)
            gproj_ref[at_k] = (scale * dot_nt(query, grad_scores)).astype(BF16)
        out_out[...] += dot_nn(att_ref[...], cot)
        qkv_out[...] += dot_nt(gproj_ref[...], scaled)
        grad_scaled = dot_nn(wq_ref[...], gproj_ref[...])
        gg_ref[...] += grad_scaled * normed
        back = normalize_back(grad_scaled * gain, normed, inv_dev, 0)
        branch_out[...] = back.T.reshape(sources, 1, each, chans).astype(BF16)

        @pl.when(step == windows - 1)
        def _():
            gain_out[...] = jnp.sum(gg_ref[...], axis=1, keepdims=True)

    by_window = pl.BlockSpec((sources, 1, each, chans), lambda step: (0, step, 0, 0))
    return pl.pallas_call(
        kernel,
        grid=(windows,),
        in_specs=[
            by_window,
            by_window,
            full((chans, 1)),
            full((chans, 3 * chans)),
            full((3 * chans, chans)),
            full((chans, chans)),
        ],
        out_specs=[
            by_window,
            full((3 * chans, chans)),
            full((chans, chans)),
            full((chans, 1)),
        ],
        out_shape=[
            jax.ShapeDtypeStruct((sources, windows, each, chans), BF16),
            jax.ShapeDtypeStruct((3 * chans, chans), F32),
            jax.ShapeDtypeStruct((chans, chans), F32),
            jax.ShapeDtypeStruct((chans, 1), F32),
        ],
        scratch_shapes=[
            pltpu.VMEM((3 * chans, length), BF16),
            pltpu.VMEM((chans, length), BF16),
            pltpu.VMEM((chans, length), BF16),
            pltpu.VMEM((3 * chans, length), BF16),
            pltpu.VMEM((chans, length), F32),
        ],
        compiler_params=params(),
        cost_estimate=cost(45),
        name="grid_attention",
    )(mid_win, cot_win, gain_col, w_qkv, w_qkv_t, w_out)


def shards(field_in, cotangent, gain_conv, w_expand, w_depth, w_project, gain_attn, w_qkv, w_out):
    rows, cols, chans = field_in.shape
    expand_w = w_expand.shape[1]
    cells = rows * cols
    row_devices = lax.axis_size("row")
    col_devices = lax.axis_size("col")
    devices = row_devices * col_devices
    grad_scale = (cells * devices) ** (-0.5)
    per_row = GRID // row_devices
    per_col = GRID // col_devices
    part_rows = rows // per_row // row_devices
    part_cols = cols // per_col // col_devices

    def to_windows(tile):
        arranged = tile.reshape(
            per_row, row_devices, part_rows, per_col, col_devices, part_cols, chans
        )
        arranged = arranged.transpose(1, 4, 2, 5, 0, 3, 6).reshape(
            devices, part_rows * part_cols, per_row * per_col, chans
        )
        return lax.all_to_all(arranged, ("row", "col"), split_axis=0, concat_axis=0, tiled=True)

    core = field_in.reshape(cells, chans)
    taps = w_depth.reshape(9, expand_w)
    above, below, left, right, _ = halo(field_in)
    middle = jnp.concatenate([above, field_in, below], axis=0)
    gap = jnp.zeros((rows + 2, EDGE - 2, chans), BF16)
    ext = jnp.concatenate([middle, right, gap, left], axis=1).reshape(-1, chans)
    held, ext = lax.optimization_barrier((cotangent, ext))
    cot_win = to_windows(held)
    hidden, acted, slope_conv, slope_pre, mid = conv_forward(
        ext, core, gain_conv.reshape(1, chans), w_expand, taps, w_project, rows, cols
    )
    mid_win = to_windows(mid.reshape(rows, cols, chans))
    branch_win, grad_qkv_t, grad_out, grad_gain_attn = grid_attention(
        mid_win, cot_win, gain_attn.reshape(chans, 1), w_qkv, w_qkv.T, w_out
    )
    grad_qkv_t, grad_out = lax.psum((grad_qkv_t, grad_out), ("row", "col"))
    moved = lax.all_to_all(branch_win, ("row", "col"), split_axis=0, concat_axis=0, tiled=True)
    moved = moved.reshape(
        row_devices, col_devices, part_rows, part_cols, per_row, per_col, chans
    )
    branch = moved.transpose(4, 0, 2, 5, 1, 3, 6).reshape(cells, chans)
    grad_conv, grad_mid, grad_mid_t = conv_grad(
        cotangent.reshape(cells, chans), branch, w_project, slope_conv
    )
    above, below, left, right, first = halo(grad_conv.reshape(rows, cols, expand_w))
    grad_project_t = project_grad(acted, grad_mid_t)
    held, _ = lax.optimization_barrier((hidden, first))
    grad_depth = depth_grad(held, grad_conv, rows, cols)
    line_pair = jnp.concatenate([above, below], axis=0)
    gap = jnp.zeros((rows + 2, EDGE - 1, expand_w), BF16)
    side_pair = jnp.concatenate([gap, left, right, gap], axis=1)
    grad_expand, grad_gain_conv, grad_field = conv_back(
        grad_conv, line_pair, side_pair, slope_pre, w_expand, taps, core,
        gain_conv.reshape(1, chans), grad_mid, rows, cols,
    )
    small_rows = 9 * expand_w // chans
    small = jnp.concatenate(
        [
            grad_depth.reshape(small_rows, chans),
            grad_gain_conv,
            grad_gain_attn.reshape(1, chans),
            jnp.zeros((-(small_rows + 2) % 8, chans), F32),
        ]
    )
    grad_expand, grad_project, small = sum_over_devices(
        grad_expand, grad_project_t, small, grad_scale
    )
    return (
        grad_field.reshape(rows, cols, chans),
        small[small_rows],
        grad_expand,
        small[:small_rows].reshape(3, 3, expand_w),
        grad_project,
        small[small_rows + 1],
        grad_qkv_t.T * grad_scale,
        grad_out * grad_scale,
    )


def sum_over_devices(expand, project_t, small, grad_scale):
    lanes = 128
    chans = expand.shape[1]
    halves = chans // lanes
    parts = (expand, project_t, small)
    starts = [0]
    for part in parts:
        starts.append(starts[-1] + part.shape[0])
    blocks = expand.shape[0] // chans
    sizes = {axis: lax.axis_size(axis) for axis in ("row", "col")}
    devices = sizes["row"] * sizes["col"]
    unit = 16 * devices
    total = -(-starts[-1] // unit) * unit
    row_bits = [("row", bit) for bit in range(sizes["row"].bit_length() - 1)]
    col_bits = [("col", bit) for bit in range(sizes["col"].bit_length() - 1)]
    orders = [row_bits + col_bits, row_bits[:1] + col_bits + row_bits[1:]]
    count = len(orders[0])

    def kernel(
        ex_ref, pr_ref, sm_ref, ex_out, pr_out, sm_out,
        acc_ref, send_ref, recv_ref, got_ref, send_sem, recv_sem,
    ):
        places = {"row": lax.axis_index("row"), "col": lax.axis_index("col")}

        def partner(axis, bit):
            mine = lax.rem(places[axis] // (1 << bit), 2)
            return mine, {axis: places[axis] + (1 - 2 * mine) * (1 << bit)}

        barrier = pltpu.get_barrier_semaphore()
        for axis, bit in orders[0]:
            _, target = partner(axis, bit)
            pl.semaphore_signal(
                barrier, inc=1, device_id=target, device_id_type=pl.DeviceIdType.MESH
            )
        pl.semaphore_wait(barrier, count)

        for lane in range(halves):
            span = slice(lane * lanes, (lane + 1) * lanes)
            for start, ref in zip(starts, (ex_ref, pr_ref, sm_ref)):
                acc_ref[lane, start : start + ref.shape[0]] = ref[:, span]
            if total > starts[-1]:
                acc_ref[lane, starts[-1] : total] = jnp.zeros((total - starts[-1], lanes), F32)

        offsets = [0] * halves

        def reduce_start(lane, step):
            size = total >> (step + 1)
            mine, target = partner(*orders[lane % 2][step])
            away = pl.multiple_of(offsets[lane] + (1 - mine) * size, 16)
            offsets[lane] = pl.multiple_of(offsets[lane] + mine * size, 16)
            send_ref[lane, pl.ds(away, size)] = acc_ref[lane, pl.ds(away, size)].astype(BF16)
            copy = pltpu.make_async_remote_copy(
                src_ref=send_ref.at[lane, pl.ds(away, size)],
                dst_ref=recv_ref.at[lane, pl.ds(total - 2 * size, size)],
                send_sem=send_sem.at[lane, step],
                recv_sem=recv_sem.at[lane, step],
                device_id=target,
                device_id_type=pl.DeviceIdType.MESH,
            )
            copy.start()
            return copy

        def reduce_end(lane, step, copy):
            size = total >> (step + 1)
            copy.wait()
            kept = pl.ds(offsets[lane], size)
            acc_ref[lane, kept] += recv_ref[lane, pl.ds(total - 2 * size, size)].astype(F32)

        copies = [reduce_start(lane, 0) for lane in range(halves)]
        for step in range(count):
            for lane in range(halves):
                reduce_end(lane, step, copies[lane])
                if step + 1 < count:
                    copies[lane] = reduce_start(lane, step + 1)

        def gather_start(lane, step):
            size = total >> (step + 1)
            mine, target = partner(*orders[lane % 2][step])
            own = pl.ds(offsets[lane], size)
            copy = pltpu.make_async_remote_copy(
                src_ref=got_ref.at[lane, own],
                dst_ref=got_ref.at[lane, own],
                send_sem=send_sem.at[lane, count + step],
                recv_sem=recv_sem.at[lane, count + step],
                device_id=target,
                device_id_type=pl.DeviceIdType.MESH,
            )
            copy.start()
            offsets[lane] = pl.multiple_of(offsets[lane] - mine * size, 16)
            return copy

        for lane in range(halves):
            own = pl.ds(offsets[lane], total >> count)
            got_ref[lane, own] = (acc_ref[lane, own] * grad_scale).astype(BF16)
            copies[lane] = gather_start(lane, count - 1)
        for step in reversed(range(count)):
            for lane in range(halves):
                copies[lane].wait()
                if step:
                    copies[lane] = gather_start(lane, step - 1)

        def read(start, size):
            return jnp.concatenate(
                [got_ref[lane, start : start + size].astype(F32) for lane in range(halves)], axis=1
            )

        for block in range(blocks):
            low, high = block * chans, (block + 1) * chans
            ex_out[:, low:high] = read(starts[0] + low, chans)
            pr_out[low:high] = read(starts[1] + low, chans).T
        packed = -(-small.shape[0] // 16) * 16
        sm_out[...] = read(starts[2], packed)[: small.shape[0]]

    whole = [pl.BlockSpec(memory_space=pltpu.VMEM)] * 3
    return pl.pallas_call(
        kernel,
        in_specs=whole,
        out_specs=whole,
        out_shape=[
            jax.ShapeDtypeStruct((chans, blocks * chans), F32),
            jax.ShapeDtypeStruct((blocks * chans, chans), F32),
            jax.ShapeDtypeStruct(small.shape, F32),
        ],
        scratch_shapes=[
            pltpu.VMEM((halves, total, lanes), F32),
            pltpu.VMEM((halves, total, lanes), BF16),
            pltpu.VMEM((halves, total, lanes), BF16),
            pltpu.VMEM((halves, total, lanes), BF16),
            pltpu.SemaphoreType.DMA((halves, 2 * count)),
            pltpu.SemaphoreType.DMA((halves, 2 * count)),
        ],
        compiler_params=pltpu.CompilerParams(
            collective_id=0, has_side_effects=True, vmem_limit_bytes=VMEM_BYTES
        ),
        name="sum_over_devices",
    )(*parts)


def solution(mesh):
    in_specs = (P("row", "col", None), P("row", "col", None), P(), P(), P(), P(), P(), P(), P())
    out_specs = (P("row", "col", None), P(), P(), P(), P(), P(), P(), P())
    return jax.shard_map(shards, mesh=mesh, in_specs=in_specs, out_specs=out_specs, check_vma=False)
```
